32 devices in a mesh: grp: 2 (over x), seq: 8 (over z, core), dp: 2 (over y).
Axes of the slice: x: 2, y: 2, z: 4, core: 2. Of those that a mesh axis runs over, the one named last changes fastest.
Arguments:
- counts: int32 [2, 8, 2, 256, 1024], P('dp', 'seq', 'grp'), may hold values from 0 to 23
- valid_frames: int32 [2, 1], replicated, may hold values from 2 to 16, as said below
- cotangent: bfloat16 [2, 16, 256, 1024], P('dp', 'seq'), may hold values from -0.125 to 0.125
- pillar_proj: bfloat16 [1024, 1024], replicated, may hold values from -0.1875 to 0.1875
- pillar_gain: float32 [1024], replicated, may hold values from 0.1 to 1.9
- latent_proj: bfloat16 [1024, 1024], replicated, may hold values from -0.1875 to 0.1875
- input_proj: bfloat16 [1024, 1024], replicated, may hold values from -0.1875 to 0.1875
- space_gain: float32 [1024], replicated, may hold values from 0.1 to 1.9
- space_project: bfloat16 [1024, 3072], replicated, may hold values from -0.1875 to 0.1875
- space_output: bfloat16 [1024, 1024], replicated, may hold values from -0.1875 to 0.1875
- time_gain: float32 [1024], replicated, may hold values from 0.1 to 1.9
- time_project: bfloat16 [1024, 3072], replicated, may hold values from -0.1875 to 0.1875
- time_output: bfloat16 [1024, 1024], replicated, may hold values from -0.75 to 0.75
Outputs:
- pillar_grad: float32 [1024, 1024], P(('grp', 'seq', 'dp'))
- latent_grad: float32 [1024, 1024], P(('grp', 'seq', 'dp'))
The draws below stay inside these ranges and needn't reach their ends.
Inputs may be any that keep to these rules, and one draw needn't show every extreme that they name: `valid_frames`: exactly one scene has all 16 frames valid.
All inputs are finite; a program needn't handle non-finite values.
Results may differ from the reference program's by a relative error of at most 0.0095.
Values may be sent and summed in bfloat16 or wider, within the bound.
A program may use at most 128 MiB of HBM per device.

```python
import math
import jax
import jax.numpy as jnp
import numpy as np
from jax import lax

LAT = 1024
D = 1024
HEADS = 8
INNER = 1024
PIN = 1024
HT = 1024
FRAMES = 16
P_SIZE = 256
SCN = 1
SFG = 16
PAIRS = 8
GROUPS = 2


def draw_valid_frames(key, part):
    total = GROUPS * SCN
    drawn = jax.random.randint(jax.random.fold_in(key, 11), (total,), 2, FRAMES)
    full_index = jax.random.randint(jax.random.fold_in(key, 12), (), 0, total)
    drawn = jnp.where(jnp.arange(total) == full_index, FRAMES, drawn)
    return drawn.reshape(GROUPS, SCN).astype(jnp.int32)


def set_ends(result, stream_key, least, top_value):
    longest = result.shape.index(max(result.shape))
    spots = []
    for shift in (0, 1):
        where = [jax.random.randint(jax.random.fold_in(stream_key, axis), (), 0, length) for axis, length in enumerate(result.shape)]
        where[longest] = (where[longest] + shift) % result.shape[longest]
        spots.append(tuple(where))
    return result.at[spots[0]].set(least).at[spots[1]].set(top_value)


def block_scale(stream_key, dims, pieces, low, high):
    level, own = 1.0, jax.random.fold_in(stream_key, 6)
    for dim, parts in pieces:
        heights = jnp.exp(jax.random.uniform(jax.random.fold_in(own, dim), (parts,), jnp.float32, low / len(pieces), high / len(pieces)))
        level = level * jnp.repeat(heights, dims[dim] // parts).reshape([-1 if axis == dim else 1 for axis in range(len(dims))])
    return level


def cumulative_ranks(amount, lean):
    loads = [(1 << 20) // math.isqrt(rank ** lean) + 1 for rank in range(1, amount + 1)]
    width = 1 + sum(loads) // (1 << 30)
    return np.cumsum(np.array([max(1, weight // width) for weight in loads]))


def ranked_ids(stream_key, shape, amount, slope):
    table = cumulative_ranks(amount, slope)
    ticket = jax.random.randint(jax.random.fold_in(stream_key, 1), shape, 0, int(table[amount - 1]))
    grade = jnp.searchsorted(jnp.asarray(table, jnp.int32), ticket, side="right")
    return jax.random.permutation(jax.random.fold_in(stream_key, 2), amount)[grade].astype(jnp.int32)


def gaussian(key, extent, deviation, reach, shards=(), kind=jnp.bfloat16):
    entries = deviation * jax.random.normal(key, extent, jnp.float32)
    if shards:
        entries = entries * block_scale(key, extent, shards, -0.22, 0.18)
    return jnp.clip(entries, -reach, reach).astype(kind)


def setup_inputs(seed: int = 0) -> dict:
    seeds = jax.random.split(jax.random.key(seed), 14)
    return {
        "counts": set_ends(ranked_ids(seeds[0], (GROUPS, PAIRS, 2, P_SIZE, PIN), 24, 2), jax.random.fold_in(seeds[0], 3), 0, 23).astype(jnp.int32),
        "valid_frames": draw_valid_frames(jax.random.fold_in(seeds[13], 71), 0),
        "cotangent": gaussian(seeds[2], (GROUPS, SFG, P_SIZE, D), 0.02, 0.125, ((0, 2), (1, 8))),
        "pillar_proj": gaussian(seeds[3], (PIN, HT), PIN ** -0.5, 0.1875),
        "pillar_gain": jnp.clip(1.0 + 0.18 * jax.random.normal(seeds[4], (HT,), jnp.float32), 0.1, 1.9),
        "latent_proj": gaussian(seeds[5], (HT, LAT), HT ** -0.5, 0.1875),
        "input_proj": gaussian(seeds[6], (LAT, D), LAT ** -0.5, 0.1875),
        "space_gain": jnp.clip(1.0 + 0.18 * jax.random.normal(seeds[7], (D,), jnp.float32), 0.1, 1.9),
        "space_project": gaussian(seeds[8], (D, 3 * INNER), D ** -0.5, 0.1875),
        "space_output": gaussian(seeds[9], (INNER, D), INNER ** -0.5, 0.1875),
        "time_gain": jnp.clip(1.0 + 0.18 * jax.random.normal(seeds[10], (D,), jnp.float32), 0.1, 1.9),
        "time_project": gaussian(seeds[11], (D, 3 * INNER), D ** -0.5, 0.1875),
        "time_output": gaussian(seeds[12], (INNER, D), (INNER // 16) ** -0.5, 0.75),
    }


def scaled_norm(values, norm_gain):
    return values * lax.rsqrt(lax.optimization_barrier(jnp.mean(values * values, axis=-1, keepdims=True)) + 1e-06) * norm_gain

def head_norm(values):
    values = values.astype(jnp.float32)
    return (values * lax.rsqrt(lax.optimization_barrier(jnp.mean(values * values, axis=-1, keepdims=True)) + 1e-06)).astype(jnp.bfloat16)

def project(activations, weight):
    return jnp.dot(activations, weight, preferred_element_type=jnp.float32)

def split_heads(joined, head_count):
    shaped = joined.reshape(joined.shape[:-1] + (3, head_count, joined.shape[-1] // (3 * head_count)))
    return (head_norm(shaped[..., 0, :, :]), head_norm(shaped[..., 1, :, :]), shaped[..., 2, :, :])

def space_core(joined, head_count):
    queries, keys, values = split_heads(joined, head_count)
    score_scale = queries.shape[-1] ** (-0.5)
    scores = jnp.einsum('grphd,grqhd->grhpq', queries.astype(jnp.float32), keys.astype(jnp.float32)) * score_scale
    weights = jnp.exp(scores)
    weights = (weights / lax.optimization_barrier(jnp.sum(weights, axis=-1, keepdims=True))).astype(jnp.bfloat16)
    mixture = jnp.einsum('grhpq,grqhd->grphd', weights.astype(jnp.float32), values.astype(jnp.float32))
    return mixture.astype(jnp.bfloat16).reshape(joined.shape[:-1] + (-1,))

def time_core(joined, head_count, visible):
    queries, keys, values = split_heads(joined, head_count)
    score_scale = queries.shape[-1] ** (-0.5)
    scores = jnp.einsum('gsfthd,gsethd->gsthfe', queries.astype(jnp.float32), keys.astype(jnp.float32)) * score_scale
    weights = jnp.exp(scores) * visible
    weights = (weights / lax.optimization_barrier(jnp.sum(weights, axis=-1, keepdims=True))).astype(jnp.bfloat16)
    mixture = jnp.einsum('gsthfe,gsethd->gsfthd', weights.astype(jnp.float32), values.astype(jnp.float32))
    return mixture.astype(jnp.bfloat16).reshape(joined.shape[:-1] + (-1,))

def mixer_inputs(residual, norm_gain, weight):
    return project(scaled_norm(residual, norm_gain).astype(jnp.bfloat16), weight).astype(jnp.bfloat16)

def space_layer(stream, norm_gain, weight_in, weight_out, head_count):
    residual = stream.astype(jnp.float32)
    joined = mixer_inputs(residual, norm_gain, weight_in)
    return (residual + project(space_core(joined, head_count), weight_out)).astype(jnp.bfloat16)

def time_layer(stream, norm_gain, weight_in, weight_out, head_count, visible):
    residual = stream.astype(jnp.float32)
    joined = mixer_inputs(residual, norm_gain, weight_in)
    return residual + project(time_core(joined, head_count, visible), weight_out)

def visibility(valid_rows, frame_count):
    position = jnp.arange(frame_count, dtype=jnp.int32)
    causal = position[None, :] <= position[:, None]
    allowed = causal[None, None] & (position[None, None, None, :] < valid_rows[:, :, None, None])
    return allowed.astype(jnp.float32)[:, :, None, None]

def activation(inputs, norm_gain):
    return jax.nn.gelu(scaled_norm(inputs, norm_gain))

def reference(counts, valid_frames, cotangent, pillar_proj, pillar_gain, latent_proj, input_proj, space_gain, space_project, space_output, time_gain, time_project, time_output):
    features = jnp.log1p(counts.astype(jnp.float32)).astype(jnp.bfloat16)
    before = project(features, pillar_proj)
    hidden, activation_back = jax.vjp(lambda inputs: activation(inputs, pillar_gain), before)
    hidden = hidden.astype(jnp.bfloat16)
    latents = project(hidden, latent_proj).astype(jnp.bfloat16).reshape(GROUPS, SFG, P_SIZE, LAT)
    visible = visibility(valid_frames, FRAMES)

    def single_frame(stream):
        return space_layer(stream, space_gain, space_project, space_output, HEADS)

    def world(latent_in):
        stream = project(latent_in, input_proj).astype(jnp.bfloat16)
        framed = lax.map(single_frame, stream.reshape(GROUPS * SFG, 1, 1, P_SIZE, D))
        return time_layer(framed.reshape(GROUPS, SCN, FRAMES, P_SIZE, D), time_gain, time_project, time_output, HEADS, visible)
    unused, world_back = jax.vjp(world, latents)
    stream_grad = world_back(cotangent.reshape(GROUPS, SCN, FRAMES, P_SIZE, D).astype(jnp.float32))[0]
    token_grad = stream_grad.reshape(GROUPS, PAIRS, 2, P_SIZE, LAT)
    hidden_grad = jnp.einsum('abcpl,hl->abcph', token_grad.astype(jnp.float32), latent_proj.astype(jnp.float32))
    before_grad = activation_back(hidden_grad)[0].astype(jnp.bfloat16)
    latent_sum = jnp.einsum('th,tl->hl', hidden.reshape(-1, HT).astype(jnp.float32), token_grad.reshape(-1, LAT).astype(jnp.float32))
    pillar_sum = jnp.einsum('tp,th->ph', features.reshape(-1, PIN).astype(jnp.float32), before_grad.reshape(-1, HT).astype(jnp.float32))
    return (pillar_sum, latent_sum)
```

```python
import functools

import jax
import jax.numpy as jnp
from jax import lax
from jax.experimental import pallas as pl
from jax.experimental.pallas import tpu as pltpu
from jax.sharding import PartitionSpec as P

CHUNKS = 2
HEADS = 8
FRAMES = 16


MESH = pl.DeviceIdType.MESH


def bit_axes(sizes):
    digits = []
    for name, size in sizes:
        weight = size // 2
        while weight:
            digits.append((name, weight))
            weight //= 2
    return digits


def halving_orders(digits):
    core = ("seq", 1)
    rest = [digit for digit in reversed(digits) if digit[0] == "seq" and digit != core]
    grp = [digit for digit in digits if digit[0] == "grp"]
    dp = [digit for digit in digits if digit[0] == "dp"]
    first = [core] if core in digits else []
    return (first + grp + dp + rest, first + dp + grp + rest)


def own_bit(digit):
    return lax.rem(lax.div(lax.axis_index(digit[0]), digit[1]), 2)


def partner(digit):
    name, weight = digit
    return {name: lax.axis_index(name) + (1 - 2 * own_bit(digit)) * weight}


def buffer_shapes(digits, rows, columns):
    return [
        (2,) * (len(digits) - 1 - stage) + (rows, columns) for stage in range(len(digits))
    ]


def greet(partners):
    barrier = pltpu.get_barrier_semaphore()
    for device in partners:
        pl.semaphore_signal(barrier, inc=1, device_id=device, device_id_type=MESH)
    pl.semaphore_wait(barrier, len(partners))


class Halving:
    def __init__(self, digits, order, chunks, part, sums, landed, out, send_sem, recv_sem):
        self.digits, self.order, self.chunks = digits, order, chunks
        self.levels = [part] + list(sums)
        self.landed, self.out = landed, out
        self.send_sem, self.recv_sem = send_sem, recv_sem
        self.width = part.shape[-1] // chunks
        self.places, left = [], list(digits)
        for digit in order:
            self.places.append(left.index(digit))
            left.remove(digit)

    def where(self, stage, chunk, bit):
        ahead = self.places[stage]
        behind = len(self.digits) - stage - 1 - ahead
        columns = pl.ds(chunk * self.width, self.width)
        index = (slice(None),) * ahead
        index += () if bit is None else (bit,)
        return index + (slice(None),) * (behind + 1) + (columns,)

    def copy(self, stage, chunk):
        digit = self.order[stage]
        return pltpu.make_async_remote_copy(
            src_ref=self.levels[stage].at[self.where(stage, chunk, 1 - own_bit(digit))],
            dst_ref=self.landed[stage].at[self.where(stage, chunk, None)],
            send_sem=self.send_sem.at[stage, chunk],
            recv_sem=self.recv_sem.at[stage, chunk],
            device_id=partner(digit),
            device_id_type=MESH,
        )

    def start(self, stage, chunk):
        self.copy(stage, chunk).start()

    def take(self, stage, chunk):
        self.copy(stage, chunk).wait_recv()
        kept = self.levels[stage][self.where(stage, chunk, own_bit(self.order[stage]))]
        place = self.where(stage, chunk, None)
        total = kept.astype(jnp.float32) + self.landed[stage][place].astype(jnp.float32)
        if stage + 1 < len(self.order):
            self.levels[stage + 1][place] = total.astype(jnp.bfloat16)
            self.start(stage + 1, chunk)
        else:
            self.out[place] = total

    def finish(self):
        for stage in range(len(self.order)):
            for chunk in range(self.chunks):
                self.copy(stage, chunk).wait_send()


def sum_kernel(digits, part_a, part_b, out_a, out_b, *scratch):
    stages = len(digits)
    sums_a, sums_b = scratch[: stages - 1], scratch[stages - 1 : 2 * stages - 2]
    rest = scratch[2 * stages - 2 :]
    landed_a, landed_b = rest[:stages], rest[stages : 2 * stages]
    send_a, recv_a, send_b, recv_b = rest[2 * stages :]
    orders = halving_orders(digits)
    both = (
        Halving(digits, orders[0], CHUNKS, part_a, sums_a, landed_a, out_a, send_a, recv_a),
        Halving(digits, orders[1], CHUNKS, part_b, sums_b, landed_b, out_b, send_b, recv_b),
    )
    greet([partner(digit) for digit in digits])
    for chunk in range(CHUNKS):
        for one in both:
            one.start(0, chunk)
    for stage in range(stages):
        for chunk in range(CHUNKS):
            for one in both:
                one.take(stage, chunk)
    for one in both:
        one.finish()


def sum_shards(part_a, part_b, sizes):
    digits = bit_axes(sizes)
    rows, columns = part_a.shape[0] >> len(digits), part_a.shape[1]
    shapes = buffer_shapes(digits, rows, columns)
    shaped = (2,) * len(digits) + (rows, columns)
    sums = [pltpu.VMEM(shape, jnp.bfloat16) for shape in shapes[:-1]]
    landed = [pltpu.VMEM(shape, jnp.bfloat16) for shape in shapes]
    sems = [pltpu.SemaphoreType.DMA((len(digits), CHUNKS))] * 4
    vmem = pl.BlockSpec(memory_space=pltpu.VMEM)
    return pl.pallas_call(
        functools.partial(sum_kernel, digits),
        out_shape=[jax.ShapeDtypeStruct((rows, columns), jnp.float32)] * 2,
        in_specs=[vmem] * 2,
        out_specs=[vmem] * 2,
        scratch_shapes=sums * 2 + landed * 2 + sems,
        compiler_params=pltpu.CompilerParams(
            collective_id=0, has_side_effects=True, vmem_limit_bytes=40 << 20
        ),
    )(
        part_a.astype(jnp.bfloat16).reshape(shaped),
        part_b.astype(jnp.bfloat16).reshape(shaped),
    )


def scaled_norm(values, norm_gain):
    return values * lax.rsqrt(jnp.mean(values * values, axis=-1, keepdims=True) + 1e-06) * norm_gain


def head_norm(values):
    values = values.astype(jnp.float32)
    return (values * lax.rsqrt(jnp.mean(values * values, axis=-1, keepdims=True) + 1e-06)).astype(
        jnp.bfloat16
    )


def project(activations, weight):
    return jnp.dot(activations, weight, preferred_element_type=jnp.float32)


def split_heads(joined, head_count):
    shaped = joined.reshape(
        joined.shape[:-1] + (3, head_count, joined.shape[-1] // (3 * head_count))
    )
    return (head_norm(shaped[..., 0, :, :]), head_norm(shaped[..., 1, :, :]), shaped[..., 2, :, :])


def space_core(joined, head_count):
    queries, keys, values = split_heads(joined, head_count)
    score_scale = queries.shape[-1] ** (-0.5)
    scores = (
        jnp.einsum("grphd,grqhd->grhpq", queries, keys, preferred_element_type=jnp.float32)
        * score_scale
    )
    weights = jnp.exp(scores)
    weights = (weights / jnp.sum(weights, axis=-1, keepdims=True)).astype(jnp.bfloat16)
    mixture = jnp.einsum("grhpq,grqhd->grphd", weights, values, preferred_element_type=jnp.float32)
    return mixture.astype(jnp.bfloat16).reshape(joined.shape[:-1] + (-1,))


def time_core(joined, head_count, visible):
    queries, keys, values = split_heads(joined, head_count)
    score_scale = queries.shape[-1] ** (-0.5)
    scores = (
        jnp.einsum("gsfthd,gsethd->gsthfe", queries, keys, preferred_element_type=jnp.float32)
        * score_scale
    )
    weights = jnp.exp(scores) * visible
    weights = (weights / jnp.sum(weights, axis=-1, keepdims=True)).astype(jnp.bfloat16)
    mixture = jnp.einsum(
        "gsthfe,gsethd->gsfthd", weights, values, preferred_element_type=jnp.float32
    )
    return mixture.astype(jnp.bfloat16).reshape(joined.shape[:-1] + (-1,))


def mixer_inputs(residual, norm_gain, weight):
    return project(scaled_norm(residual, norm_gain).astype(jnp.bfloat16), weight).astype(
        jnp.bfloat16
    )


def space_layer(stream, norm_gain, weight_in, weight_out, head_count):
    residual = stream.astype(jnp.float32)
    joined = mixer_inputs(residual, norm_gain, weight_in)
    return (residual + project(space_core(joined, head_count), weight_out)).astype(jnp.bfloat16)


def time_layer(stream, norm_gain, weight_in, weight_out, head_count, visible):
    residual = stream.astype(jnp.float32)
    joined = mixer_inputs(residual, norm_gain, weight_in)
    return residual + project(time_core(joined, head_count, visible), weight_out)


def visibility(valid_rows, frame_count):
    position = jnp.arange(frame_count, dtype=jnp.int32)
    causal = position[None, :] <= position[:, None]
    allowed = causal[None, None] & (position[None, None, None, :] < valid_rows[:, :, None, None])
    return allowed.astype(jnp.float32)[:, :, None, None]


def activation(inputs, norm_gain):
    return jax.nn.gelu(scaled_norm(inputs, norm_gain))


def frame_order(values):
    count = values.shape[1]
    shaped = values.reshape((1, 2, count // 2) + values.shape[2:])
    return jnp.swapaxes(shaped, 1, 2).reshape(values.shape)


def side_order(values):
    count = values.shape[1]
    shaped = values.reshape((1, count // 2, 2) + values.shape[2:])
    return jnp.swapaxes(shaped, 1, 2).reshape(values.shape)


def shards(
    sizes,
    counts,
    valid_frames,
    cotangent,
    pillar_proj,
    pillar_gain,
    latent_proj,
    input_proj,
    space_gain,
    space_project,
    space_output,
    time_gain,
    time_project,
    time_output,
):
    group_side = lax.axis_index("grp")
    features = jnp.log1p(counts.astype(jnp.float32)).astype(jnp.bfloat16)
    features = features.reshape(1, 1, features.shape[3], features.shape[4])

    def tokenize(pillars):
        before = project(pillars, pillar_proj)
        hidden, activation_back = jax.vjp(lambda inputs: activation(inputs, pillar_gain), before)
        hidden = hidden.astype(jnp.bfloat16)
        return (project(hidden, latent_proj).astype(jnp.bfloat16), hidden, activation_back)

    latents, hidden, activation_back = tokenize(features)
    pillars = features
    own_cot = lax.dynamic_slice_in_dim(cotangent, group_side, 1, 1)

    def front_part(latent_in):
        stream = project(latent_in, input_proj).astype(jnp.bfloat16)
        return space_layer(stream, space_gain, space_project, space_output, HEADS)

    spatial_out, front_back = jax.vjp(front_part, latents)
    scenes = valid_frames.shape[1]
    visible = visibility(lax.dynamic_slice_in_dim(valid_frames, lax.axis_index("dp"), 1, 0), FRAMES)
    tile_stream = frame_order(
        lax.all_to_all(spatial_out, ("grp", "seq"), split_axis=2, concat_axis=1, tiled=True)
    )
    tile_cotangent = frame_order(
        lax.all_to_all(own_cot, ("grp", "seq"), split_axis=2, concat_axis=1, tiled=True)
    )
    tile_count = tile_stream.shape[2]

    def whole_layer(stream):
        return time_layer(
            stream.reshape(1, scenes, FRAMES, tile_count, -1),
            time_gain,
            time_project,
            time_output,
            HEADS,
            visible,
        )

    unused, layer_back = jax.vjp(whole_layer, tile_stream)
    tile_grad = layer_back(
        tile_cotangent.reshape(1, scenes, FRAMES, tile_count, -1).astype(jnp.float32)
    )[0]
    spatial_grad = lax.all_to_all(
        side_order(tile_grad), ("grp", "seq"), split_axis=1, concat_axis=2, tiled=True
    )
    stream_grad = front_back(spatial_grad)[0]
    kept_share = jnp.float32(1.0)
    hidden_flat = hidden.reshape(-1, hidden.shape[-1])
    grad_flat = stream_grad.reshape(-1, stream_grad.shape[-1])
    latent_part = (
        jnp.einsum("th,tl->hl", hidden_flat, grad_flat, preferred_element_type=jnp.float32)
        * kept_share
    )
    hidden_grad = jnp.einsum(
        "grpl,hl->grph", stream_grad, latent_proj, preferred_element_type=jnp.float32
    )
    before_grad = activation_back(hidden_grad)[0].astype(jnp.bfloat16)
    pillar_flat = pillars.reshape(-1, pillars.shape[-1])
    before_flat = before_grad.reshape(-1, before_grad.shape[-1])
    pillar_part = (
        jnp.einsum("tp,th->ph", pillar_flat, before_flat, preferred_element_type=jnp.float32)
        * kept_share
    )
    latent_sum, pillar_sum = sum_shards(latent_part, pillar_part, sizes)
    return pillar_sum, latent_sum


def solution(mesh):
    placed = (
        P("dp", "seq", "grp", None, None),
        P(),
        P("dp", "seq", None, None),
        P(),
        P(),
        P(),
        P(),
        P(),
        P(),
        P(),
        P(),
        P(),
        P(),
    )
    return jax.shard_map(
        functools.partial(shards, tuple(mesh.shape.items())),
        mesh=mesh,
        in_specs=placed,
        out_specs=(P(("grp", "seq", "dp"), None), P(("grp", "seq", "dp"), None)),
        check_vma=False,
    )
```

```python
import functools

import jax
import jax.numpy as jnp
from jax import lax
from jax.experimental import pallas as pl
from jax.experimental.pallas import tpu as pltpu
from jax.sharding import PartitionSpec as P

CHUNKS = 2
HEADS = 8
FRAMES = 16
ROWS = 32
TILE = 256
GELU = (2.0 / 3.141592653589793) ** 0.5
MESH = pl.DeviceIdType.MESH


def bit_axes(sizes):
    digits = []
    for name, size in sizes:
        weight = size // 2
        while weight:
            digits.append((name, weight))
            weight //= 2
    return digits


def halving_orders(digits):
    core = ("seq", 1)
    rest = [digit for digit in reversed(digits) if digit[0] == "seq" and digit != core]
    grp = [digit for digit in digits if digit[0] == "grp"]
    dp = [digit for digit in digits if digit[0] == "dp"]
    first = [core] if core in digits else []
    return (first + grp + dp + rest, first + dp + grp + rest)


def own_bit(digit):
    return lax.rem(lax.div(lax.axis_index(digit[0]), digit[1]), 2)


def partner(digit):
    name, weight = digit
    return {name: lax.axis_index(name) + (1 - 2 * own_bit(digit)) * weight}


def buffer_shapes(digits, rows, columns):
    return [
        (2,) * (len(digits) - 1 - stage) + (rows, columns) for stage in range(len(digits))
    ]


class Halving:
    def __init__(self, digits, order, chunks, part, sums, landed, out, send_sem, recv_sem):
        self.digits, self.order, self.chunks = digits, order, chunks
        self.levels = [part] + list(sums)
        self.landed, self.out = landed, out
        self.send_sem, self.recv_sem = send_sem, recv_sem
        self.width = part.shape[-1] // chunks
        self.places, left = [], list(digits)
        for digit in order:
            self.places.append(left.index(digit))
            left.remove(digit)

    def where(self, stage, chunk, bit):
        ahead = self.places[stage]
        behind = len(self.digits) - stage - 1 - ahead
        columns = pl.ds(chunk * self.width, self.width)
        index = (slice(None),) * ahead
        index += () if bit is None else (bit,)
        return index + (slice(None),) * (behind + 1) + (columns,)

    def copy(self, stage, chunk):
        digit = self.order[stage]
        return pltpu.make_async_remote_copy(
            src_ref=self.levels[stage].at[self.where(stage, chunk, 1 - own_bit(digit))],
            dst_ref=self.landed[stage].at[self.where(stage, chunk, None)],
            send_sem=self.send_sem.at[stage, chunk],
            recv_sem=self.recv_sem.at[stage, chunk],
            device_id=partner(digit),
            device_id_type=MESH,
        )

    def start(self, stage, chunk):
        self.copy(stage, chunk).start()

    def take(self, stage, chunk):
        self.copy(stage, chunk).wait_recv()
        kept = self.levels[stage][self.where(stage, chunk, own_bit(self.order[stage]))]
        place = self.where(stage, chunk, None)
        total = kept.astype(jnp.float32) + self.landed[stage][place].astype(jnp.float32)
        if stage + 1 < len(self.order):
            self.levels[stage + 1][place] = total.astype(jnp.bfloat16)
            self.start(stage + 1, chunk)
        else:
            self.out[place] = total

    def finish(self):
        for stage in range(len(self.order)):
            for chunk in range(self.chunks):
                self.copy(stage, chunk).wait_send()


EPS = 1e-06
NT = (((1,), (1,)), ((), ()))
TN = (((0,), (0,)), ((), ()))


def contract(left, right, dims):
    return lax.dot_general(left, right, dims, preferred_element_type=jnp.float32)


def aligned(start, size):
    return pl.ds(pl.multiple_of(start, size), size)


def over(count, body):
    def step(place, carry):
        body(place)
        return carry

    lax.fori_loop(0, count, step, 0)


def over_rows(array, body):
    over(array.shape[0] // ROWS, lambda place: body(aligned(place * ROWS, ROWS)))


def times(left, weight, store):
    def tile(place):
        columns = aligned(place * TILE, TILE)
        store(columns, jnp.dot(left[...], weight[:, columns], preferred_element_type=jnp.float32))

    over(weight.shape[1] // TILE, tile)


def times_back(left, weight, store):
    def tile(place):
        columns = aligned(place * TILE, TILE)
        store(columns, contract(left[...], weight[columns, :], NT))

    over(weight.shape[0] // TILE, tile)


def into(target):
    def store(columns, value):
        target[:, columns] = value.astype(target.dtype)

    return store


def unit(values):
    values = values.astype(jnp.float32)
    scale = lax.rsqrt(jnp.mean(values * values, axis=-1, keepdims=True) + EPS)
    return values * scale, scale


def unit_back(grad, units, scale):
    return scale * (grad - units * jnp.mean(grad * units, axis=-1, keepdims=True))


def norm_rows(source, gain, target):
    def block(rows):
        target[rows, :] = (unit(source[rows, :])[0] * gain[...]).astype(jnp.bfloat16)

    over_rows(source, block)


def norm_rows_back(source, gain, grad, residual, target):
    def block(rows):
        units, scale = unit(source[rows, :])
        inner = unit_back(grad[rows, :].astype(jnp.float32) * gain[...], units, scale)
        target[rows, :] = (residual[rows, :].astype(jnp.float32) + inner).astype(jnp.bfloat16)

    over_rows(source, block)


def head_parts(joined, head):
    inner = joined.shape[1] // 3
    size = inner // HEADS
    return [aligned(part * inner + head * size, size) for part in range(3)]


def head_weights(joined, columns, mask):
    queries, query_scale = unit(joined[:, columns[0]])
    keys, key_scale = unit(joined[:, columns[1]])
    query_half, key_half = queries.astype(jnp.bfloat16), keys.astype(jnp.bfloat16)
    scores = contract(query_half, key_half, NT) * queries.shape[-1] ** (-0.5)
    weights = jnp.exp(scores)
    if mask is not None:
        weights = weights * mask[...]
    weights = weights / jnp.sum(weights, axis=-1, keepdims=True)
    return weights, (queries, query_scale, query_half), (keys, key_scale, key_half)


def attend(joined, mixed):
    def head(place):
        columns = head_parts(joined, place)
        weights = head_weights(joined, columns, None)[0].astype(jnp.bfloat16)
        mixture = jnp.dot(weights, joined[:, columns[2]], preferred_element_type=jnp.float32)
        mixed[:, columns_of(mixed, place)] = mixture.astype(jnp.bfloat16)

    over(HEADS, head)


def columns_of(mixed, place):
    size = mixed.shape[1] // HEADS
    return aligned(place * size, size)


def attend_back(joined, mixed_grad, joined_grad, mask):
    def head(place):
        columns = head_parts(joined, place)
        weights, (queries, query_scale, query_half), (keys, key_scale, key_half) = head_weights(
            joined, columns, mask
        )
        grad = mixed_grad[:, columns_of(mixed_grad, place)]
        joined_grad[:, columns[2]] = contract(weights.astype(jnp.bfloat16), grad, TN).astype(
            jnp.bfloat16
        )
        weight_grad = contract(grad, joined[:, columns[2]], NT)
        weight_grad = weight_grad.astype(jnp.bfloat16).astype(jnp.float32)
        shared = jnp.sum(weights * weight_grad, axis=-1, keepdims=True)
        score_grad = weights * (weight_grad - shared) * queries.shape[-1] ** (-0.5)
        score_grad = score_grad.astype(jnp.bfloat16)
        query_grad = jnp.dot(score_grad, key_half, preferred_element_type=jnp.float32)
        key_grad = contract(score_grad, query_half, TN)
        query_grad = query_grad.astype(jnp.bfloat16).astype(jnp.float32)
        key_grad = key_grad.astype(jnp.bfloat16).astype(jnp.float32)
        joined_grad[:, columns[0]] = unit_back(query_grad, queries, query_scale).astype(
            jnp.bfloat16
        )
        joined_grad[:, columns[1]] = unit_back(key_grad, keys, key_scale).astype(jnp.bfloat16)

    over(HEADS, head)


class Exchange:
    def __init__(self, sides, source, target, send_sem, recv_sem):
        self.sides, self.source, self.target = sides, source, target
        self.send_sem, self.recv_sem = send_sem, recv_sem
        seq, scene_seqs = lax.axis_index("seq"), FRAMES // sides
        local = lax.rem(seq, scene_seqs)
        self.base = seq - local
        self.frame = local * sides + lax.axis_index("grp")
        self.size = target.shape[0] // FRAMES

    def rows(self, frame):
        return aligned(frame * self.size, self.size)

    def device(self, frame):
        return {"grp": lax.rem(frame, self.sides), "seq": self.base + lax.div(frame, self.sides)}

    def away(self, step):
        return lax.rem(self.frame + step, FRAMES)

    def copy(self, step, to, landing):
        return pltpu.make_async_remote_copy(
            src_ref=self.source.at[self.rows(to), :],
            dst_ref=self.target.at[self.rows(landing), :],
            send_sem=self.send_sem.at[step],
            recv_sem=self.recv_sem.at[step],
            device_id=self.device(to),
            device_id_type=MESH,
        )

    def start(self):
        def one(place):
            self.copy(place + 1, self.away(place + 1), self.frame).start()

        over(FRAMES - 1, one)
        own = self.rows(self.frame)
        self.target[own, :] = self.source[own, :]

    def wait(self):
        def one(place):
            step = place + 1
            sender = lax.rem(self.frame + FRAMES - step, FRAMES)
            self.copy(step, sender, sender).wait_recv()

        over(FRAMES - 1, one)

    def finish(self):
        def one(place):
            self.copy(place + 1, self.away(place + 1), self.frame).wait_send()

        over(FRAMES - 1, one)


def visible(mask, valid, sides):
    tokens = mask.shape[0] // FRAMES
    scene = lax.div(lax.axis_index("seq"), FRAMES // sides)
    limit = valid[lax.axis_index("dp"), scene]
    query = lax.broadcasted_iota(jnp.int32, mask.shape, 0)
    key = lax.broadcasted_iota(jnp.int32, mask.shape, 1)
    query_frame, key_frame = lax.div(query, tokens), lax.div(key, tokens)
    same = query - query_frame * tokens == key - key_frame * tokens
    seen = same & (key_frame <= query_frame) & (key_frame < limit)
    mask[...] = seen.astype(jnp.float32)


def weight_part(left, right, part, chunk):
    width = right.shape[1] // CHUNKS
    columns = pl.ds(chunk * width, width)
    ahead = (left.shape[1] // TILE).bit_length() - 1
    blocks = part.shape[ahead:-2]

    def tile(place):
        value = contract(left[:, aligned(place * TILE, TILE)], right[:, columns], TN)
        value = value.reshape(blocks + (part.shape[-2], width)).astype(jnp.bfloat16)
        bits = tuple(lax.rem(lax.div(place, 1 << (ahead - 1 - i)), 2) for i in range(ahead))
        part[bits + (slice(None),) * (len(blocks) + 1) + (columns,)] = value

    over(left.shape[1] // TILE, tile)


def world_kernel(
    digits,
    sides,
    valid,
    counts,
    cotangent,
    pillar_gain,
    space_gain,
    time_gain,
    *refs,
):
    weights_far, refs = refs[:7], refs[7:]
    (pillar_out, latent_out), refs = refs[:2], refs[2:]
    weights, refs = refs[:7], refs[7:]
    weight_sem, refs = refs[0], refs[1:]
    (features, before, hidden, stream, work, joined, mixed, spaced), refs = refs[:8], refs[8:]
    (tile_stream, tile_cot, joined_grad, tile_grad, back, wide, mask, tile_joined), refs = (
        refs[:8],
        refs[8:],
    )
    ways, refs = refs[:6], refs[6:]
    stages = len(digits)
    part_a, part_b = refs[:2]
    scratch = refs[2:]
    sums_a, sums_b = scratch[: stages - 1], scratch[stages - 1 : 2 * stages - 2]
    rest = scratch[2 * stages - 2 :]
    landed_a, landed_b = rest[:stages], rest[stages : 2 * stages]
    send_a, recv_a, send_b, recv_b = rest[2 * stages :]
    orders = halving_orders(digits)
    latent_sum = Halving(
        digits, orders[0], CHUNKS, part_a, sums_a, landed_a, latent_out, send_a, recv_a
    )
    pillar_sum = Halving(
        digits, orders[1], CHUNKS, part_b, sums_b, landed_b, pillar_out, send_b, recv_b
    )
    own_cot = cotangent.at[lax.axis_index("grp")]
    cot_way = Exchange(sides, own_cot, tile_cot, ways[0], ways[1])
    stream_way = Exchange(sides, spaced, tile_stream, ways[2], ways[3])
    back_way = Exchange(sides, tile_grad, back, ways[4], ways[5])

    loads = [
        pltpu.make_async_copy(far, near, weight_sem.at[place])
        for place, (far, near) in enumerate(zip(weights_far, weights))
    ]
    for load in loads:
        load.start()

    barrier = pltpu.get_barrier_semaphore()

    def greet_frame(place):
        device = cot_way.device(cot_way.away(place + 1))
        pl.semaphore_signal(barrier, inc=1, device_id=device, device_id_type=MESH)

    over(FRAMES - 1, greet_frame)
    others = [
        digit
        for digit in digits
        if digit[0] == "dp" or (digit[0] == "seq" and digit[1] >= FRAMES // sides)
    ]
    for digit in others:
        pl.semaphore_signal(barrier, inc=1, device_id=partner(digit), device_id_type=MESH)

    def features_rows(rows):
        features[rows, :] = jnp.log(1.0 + counts[rows, :].astype(jnp.float32)).astype(jnp.bfloat16)

    over_rows(features, features_rows)
    pl.semaphore_wait(barrier, FRAMES - 1 + len(others))
    cot_way.start()

    pillar_proj, latent_proj, input_proj, space_project, space_output = weights[:5]
    time_project, time_output = weights[5:]
    loads[0].wait()
    times(features, pillar_proj, into(before))

    def hidden_rows(rows):
        inputs = unit(before[rows, :])[0] * pillar_gain[...]
        bent = jnp.tanh(GELU * (inputs + 0.044715 * inputs * inputs * inputs))
        hidden[rows, :] = (0.5 * inputs * (1.0 + bent)).astype(jnp.bfloat16)

    over_rows(hidden, hidden_rows)
    loads[1].wait()
    times(hidden, latent_proj, into(work))
    loads[2].wait()
    times(work, input_proj, into(stream))
    norm_rows(stream, space_gain, work)
    loads[3].wait()
    times(work, space_project, into(joined))
    attend(joined, mixed)
    loads[4].wait()

    def space_store(columns, value):
        spaced[:, columns] = (stream[:, columns].astype(jnp.float32) + value).astype(jnp.bfloat16)

    times(mixed, space_output, space_store)
    stream_way.start()

    visible(mask, valid, sides)
    cot_way.wait()
    loads[5].wait()
    loads[6].wait()
    times_back(tile_cot, time_output, into(mixed))
    stream_way.wait()
    norm_rows(tile_stream, time_gain, work)
    times(work, time_project, into(tile_joined))
    attend_back(tile_joined, mixed, joined_grad, mask)
    times_back(joined_grad, time_project, into(work))
    norm_rows_back(tile_stream, time_gain, work, tile_cot, tile_grad)
    back_way.start()

    back_way.wait()
    times_back(back, space_output, into(mixed))
    attend_back(joined, mixed, joined_grad, None)
    times_back(joined_grad, space_project, into(work))
    norm_rows_back(stream, space_gain, work, back, mixed)
    times_back(mixed, input_proj, into(work))
    for chunk in range(CHUNKS):
        weight_part(hidden, work, part_a, chunk)
        latent_sum.start(0, chunk)
    times_back(work, latent_proj, into(wide))

    def before_rows(rows):
        units, scale = unit(before[rows, :])
        inputs = units * pillar_gain[...]
        square = inputs * inputs
        bent = jnp.tanh(GELU * (inputs + 0.044715 * square * inputs))
        slope = 0.5 * (1.0 + bent) + 0.5 * inputs * (1.0 - bent * bent) * GELU * (
            1.0 + 3 * 0.044715 * square
        )
        grad = wide[rows, :] * slope * pillar_gain[...]
        mixed[rows, :] = unit_back(grad, units, scale).astype(jnp.bfloat16)

    over_rows(before, before_rows)
    for chunk in range(CHUNKS):
        weight_part(features, mixed, part_b, chunk)
        pillar_sum.start(0, chunk)
    for stage in range(stages):
        for chunk in range(CHUNKS):
            latent_sum.take(stage, chunk)
            pillar_sum.take(stage, chunk)
    for way in (cot_way, stream_way, back_way):
        way.finish()
    latent_sum.finish()
    pillar_sum.finish()


def shards(
    sizes,
    counts,
    valid_frames,
    cotangent,
    pillar_proj,
    pillar_gain,
    latent_proj,
    input_proj,
    space_gain,
    space_project,
    space_output,
    time_gain,
    time_project,
    time_output,
):
    digits = bit_axes(sizes)
    tokens, width = counts.shape[-2:]
    model = input_proj.shape[1]
    rows = pillar_proj.shape[0] >> len(digits)
    weights = (
        pillar_proj,
        latent_proj,
        input_proj,
        space_project,
        space_output,
        time_project,
        time_output,
    )

    def half(*shape):
        return pltpu.VMEM(shape, jnp.bfloat16)

    def full(*shape):
        return pltpu.VMEM(shape, jnp.float32)

    hidden_width, latent_width = latent_proj.shape
    joined_width = space_project.shape[1]
    shapes = buffer_shapes(digits, rows, latent_width)
    shaped = (2,) * len(digits) + (rows, latent_width)
    scratch = [half(*weight.shape) for weight in weights]
    scratch += [pltpu.SemaphoreType.DMA((len(weights),))]
    scratch += [
        half(tokens, width),
        full(tokens, hidden_width),
        half(tokens, hidden_width),
        half(tokens, model),
        half(tokens, model),
        half(tokens, joined_width),
        half(tokens, model),
        half(tokens, model),
        half(tokens, model),
        half(tokens, model),
        half(tokens, joined_width),
        half(tokens, model),
        half(tokens, model),
        full(tokens, hidden_width),
        full(tokens, tokens),
        half(tokens, joined_width),
    ]
    scratch += [pltpu.SemaphoreType.DMA((FRAMES,))] * 6
    scratch += [half(*shaped)] * 2
    scratch += [half(*shape) for shape in shapes[:-1]] * 2
    scratch += [half(*shape) for shape in shapes] * 2
    scratch += [pltpu.SemaphoreType.DMA((len(digits), CHUNKS))] * 4
    vmem = pl.BlockSpec(memory_space=pltpu.VMEM)
    far = pl.BlockSpec(memory_space=pl.ANY)
    return pl.pallas_call(
        functools.partial(world_kernel, digits, dict(sizes)["grp"]),
        out_shape=[
            jax.ShapeDtypeStruct((rows, hidden_width), jnp.float32),
            jax.ShapeDtypeStruct((rows, latent_width), jnp.float32),
        ],
        in_specs=[pl.BlockSpec(memory_space=pltpu.SMEM)] + [vmem] * 5 + [far] * len(weights),
        out_specs=[vmem] * 2,
        scratch_shapes=scratch,
        compiler_params=pltpu.CompilerParams(
            collective_id=0, has_side_effects=True, vmem_limit_bytes=58 << 20
        ),
    )(
        valid_frames,
        counts.reshape(tokens, width),
        cotangent.reshape(cotangent.shape[1:]),
        pillar_gain.reshape(1, -1),
        space_gain.reshape(1, -1),
        time_gain.reshape(1, -1),
        *weights,
    )


def solution(mesh):
    placed = (
        P("dp", "seq", "grp", None, None),
        P(),
        P("dp", "seq", None, None),
        P(),
        P(),
        P(),
        P(),
        P(),
        P(),
        P(),
        P(),
        P(),
        P(),
    )
    sizes = tuple((name, mesh.shape[name]) for name in ("grp", "seq", "dp"))
    return jax.shard_map(
        functools.partial(shards, sizes),
        mesh=mesh,
        in_specs=placed,
        out_specs=(P(("grp", "seq", "dp"), None), P(("grp", "seq", "dp"), None)),
        check_vma=False,
    )
```

```python
import functools

import jax
import jax.numpy as jnp
from jax import lax
from jax.experimental import pallas as pl
from jax.experimental.pallas import tpu as pltpu
from jax.sharding import PartitionSpec as P

CHUNKS = 2
HEADS = 8
FRAMES = 16
ROWS = 32
TILE = 256
GELU = (2.0 / 3.141592653589793) ** 0.5
MESH = pl.DeviceIdType.MESH


def bit_axes(sizes):
    digits = []
    for name, size in sizes:
        weight = size // 2
        while weight:
            digits.append((name, weight))
            weight //= 2
    return digits


def halving_orders(digits):
    core = ("seq", 1)
    rest = [digit for digit in reversed(digits) if digit[0] == "seq" and digit != core]
    grp = [digit for digit in digits if digit[0] == "grp"]
    dp = [digit for digit in digits if digit[0] == "dp"]
    first = [core] if core in digits else []
    return (first + grp + dp + rest, first + dp + grp + rest)


def own_bit(digit):
    return lax.rem(lax.div(lax.axis_index(digit[0]), digit[1]), 2)


def partner(digit):
    name, weight = digit
    return {name: lax.axis_index(name) + (1 - 2 * own_bit(digit)) * weight}


def buffer_shapes(digits, rows, columns):
    return [
        (2,) * (len(digits) - 1 - stage) + (rows, columns) for stage in range(len(digits))
    ]


class Halving:
    def __init__(self, digits, order, chunks, part, sums, landed, out, send_sem, recv_sem):
        self.digits, self.order, self.chunks = digits, order, chunks
        self.levels = [part] + list(sums)
        self.landed, self.out = landed, out
        self.send_sem, self.recv_sem = send_sem, recv_sem
        self.width = part.shape[-1] // chunks
        self.places, left = [], list(digits)
        for digit in order:
            self.places.append(left.index(digit))
            left.remove(digit)

    def where(self, stage, chunk, bit):
        ahead = self.places[stage]
        behind = len(self.digits) - stage - 1 - ahead
        columns = pl.ds(chunk * self.width, self.width)
        index = (slice(None),) * ahead
        index += () if bit is None else (bit,)
        return index + (slice(None),) * (behind + 1) + (columns,)

    def copy(self, stage, chunk):
        digit = self.order[stage]
        return pltpu.make_async_remote_copy(
            src_ref=self.levels[stage].at[self.where(stage, chunk, 1 - own_bit(digit))],
            dst_ref=self.landed[stage].at[self.where(stage, chunk, None)],
            send_sem=self.send_sem.at[stage, chunk],
            recv_sem=self.recv_sem.at[stage, chunk],
            device_id=partner(digit),
            device_id_type=MESH,
        )

    def start(self, stage, chunk):
        self.copy(stage, chunk).start()

    def take(self, stage, chunk):
        self.copy(stage, chunk).wait_recv()
        kept = self.levels[stage][self.where(stage, chunk, own_bit(self.order[stage]))]
        place = self.where(stage, chunk, None)
        total = kept.astype(jnp.float32) + self.landed[stage][place].astype(jnp.float32)
        if stage + 1 < len(self.order):
            self.levels[stage + 1][place] = total.astype(jnp.bfloat16)
            self.start(stage + 1, chunk)
        else:
            self.out[place] = total

    def finish(self):
        for stage in range(len(self.order)):
            for chunk in range(self.chunks):
                self.copy(stage, chunk).wait_send()


EPS = 1e-06
NT = (((1,), (1,)), ((), ()))
TN = (((0,), (0,)), ((), ()))


def contract(left, right, dims):
    return lax.dot_general(left, right, dims, preferred_element_type=jnp.float32)


def aligned(start, size):
    return pl.ds(pl.multiple_of(start, size), size)


def over(count, body, group=1):
    def step(place, carry):
        for member in range(group):
            body(place * group + member)
        return carry

    lax.fori_loop(0, count // group, step, 0)


def over_rows(array, body):
    over(array.shape[0] // ROWS, lambda place: body(aligned(place * ROWS, ROWS)))


def times(left, weight, store):
    def tile(place):
        columns = aligned(place * TILE, TILE)
        store(columns, jnp.dot(left[...], weight[:, columns], preferred_element_type=jnp.float32))

    over(weight.shape[1] // TILE, tile, 4)


def times_back(left, weight, store):
    def tile(place):
        columns = aligned(place * TILE, TILE)
        store(columns, contract(left[...], weight[columns, :], NT))

    over(weight.shape[0] // TILE, tile, 4)


def into(target):
    def store(columns, value):
        target[:, columns] = value.astype(target.dtype)

    return store


def unit(values):
    values = values.astype(jnp.float32)
    scale = lax.rsqrt(jnp.mean(values * values, axis=-1, keepdims=True) + EPS)
    return values * scale, scale


def unit_back(grad, units, scale):
    return scale * (grad - units * jnp.mean(grad * units, axis=-1, keepdims=True))


def norm_rows(source, gain, target):
    def block(rows):
        target[rows, :] = (unit(source[rows, :])[0] * gain[...]).astype(jnp.bfloat16)

    over_rows(source, block)


def norm_rows_back(source, gain, grad, residual, target):
    def block(rows):
        units, scale = unit(source[rows, :])
        inner = unit_back(grad[rows, :].astype(jnp.float32) * gain[...], units, scale)
        target[rows, :] = (residual[rows, :].astype(jnp.float32) + inner).astype(jnp.bfloat16)

    over_rows(source, block)


def head_parts(joined, head):
    inner = joined.shape[1] // 3
    size = inner // HEADS
    return [aligned(part * inner + head * size, size) for part in range(3)]


def head_weights(joined, columns, mask):
    queries, query_scale = unit(joined[:, columns[0]])
    keys, key_scale = unit(joined[:, columns[1]])
    query_half, key_half = queries.astype(jnp.bfloat16), keys.astype(jnp.bfloat16)
    scores = contract(query_half, key_half, NT) * queries.shape[-1] ** (-0.5)
    weights = jnp.exp(scores)
    if mask is not None:
        weights = weights * mask[...]
    weights = weights * (1.0 / jnp.sum(weights, axis=-1, keepdims=True))
    return weights, (queries, query_scale, query_half), (keys, key_scale, key_half)


def attend(joined, mixed):
    def head(place):
        columns = head_parts(joined, place)
        weights = head_weights(joined, columns, None)[0].astype(jnp.bfloat16)
        mixture = jnp.dot(weights, joined[:, columns[2]], preferred_element_type=jnp.float32)
        mixed[:, columns_of(mixed, place)] = mixture.astype(jnp.bfloat16)

    over(HEADS, head, 2)


def columns_of(mixed, place):
    size = mixed.shape[1] // HEADS
    return aligned(place * size, size)


def attend_back(joined, mixed_grad, joined_grad, mask):
    def head(place):
        columns = head_parts(joined, place)
        weights, (queries, query_scale, query_half), (keys, key_scale, key_half) = head_weights(
            joined, columns, mask
        )
        grad = mixed_grad[:, columns_of(mixed_grad, place)]
        joined_grad[:, columns[2]] = contract(weights.astype(jnp.bfloat16), grad, TN).astype(
            jnp.bfloat16
        )
        weight_grad = contract(grad, joined[:, columns[2]], NT)
        weight_grad = weight_grad.astype(jnp.bfloat16).astype(jnp.float32)
        shared = jnp.sum(weights * weight_grad, axis=-1, keepdims=True)
        score_grad = weights * (weight_grad - shared) * queries.shape[-1] ** (-0.5)
        score_grad = score_grad.astype(jnp.bfloat16)
        query_grad = jnp.dot(score_grad, key_half, preferred_element_type=jnp.float32)
        key_grad = contract(score_grad, query_half, TN)
        query_grad = query_grad.astype(jnp.bfloat16).astype(jnp.float32)
        key_grad = key_grad.astype(jnp.bfloat16).astype(jnp.float32)
        joined_grad[:, columns[0]] = unit_back(query_grad, queries, query_scale).astype(
            jnp.bfloat16
        )
        joined_grad[:, columns[1]] = unit_back(key_grad, keys, key_scale).astype(jnp.bfloat16)

    over(HEADS, head, 2)


class Exchange:
    def __init__(self, sides, source, target, send_sem, recv_sem):
        self.sides, self.source, self.target = sides, source, target
        self.send_sem, self.recv_sem = send_sem, recv_sem
        seq, scene_seqs = lax.axis_index("seq"), FRAMES // sides
        local = lax.rem(seq, scene_seqs)
        self.base = seq - local
        self.frame = local * sides + lax.axis_index("grp")
        self.size = target.shape[0] // FRAMES

    def rows(self, frame):
        return aligned(frame * self.size, self.size)

    def device(self, frame):
        return {"grp": lax.rem(frame, self.sides), "seq": self.base + lax.div(frame, self.sides)}

    def away(self, step):
        return lax.rem(self.frame + step, FRAMES)

    def copy(self, step, to, landing):
        return pltpu.make_async_remote_copy(
            src_ref=self.source.at[self.rows(to), :],
            dst_ref=self.target.at[self.rows(landing), :],
            send_sem=self.send_sem.at[step],
            recv_sem=self.recv_sem.at[step],
            device_id=self.device(to),
            device_id_type=MESH,
        )

    def start(self):
        def one(place):
            self.copy(place + 1, self.away(place + 1), self.frame).start()

        over(FRAMES - 1, one)
        own = self.rows(self.frame)
        self.target[own, :] = self.source[own, :]

    def wait(self):
        def one(place):
            step = place + 1
            sender = lax.rem(self.frame + FRAMES - step, FRAMES)
            self.copy(step, sender, sender).wait_recv()

        over(FRAMES - 1, one)

    def finish(self):
        def one(place):
            self.copy(place + 1, self.away(place + 1), self.frame).wait_send()

        over(FRAMES - 1, one)


def visible(mask, valid, sides):
    tokens = mask.shape[0] // FRAMES
    scene = lax.div(lax.axis_index("seq"), FRAMES // sides)
    limit = valid[lax.axis_index("dp"), scene]
    query = lax.broadcasted_iota(jnp.int32, mask.shape, 0)
    key = lax.broadcasted_iota(jnp.int32, mask.shape, 1)
    query_frame, key_frame = lax.div(query, tokens), lax.div(key, tokens)
    same = query - query_frame * tokens == key - key_frame * tokens
    seen = same & (key_frame <= query_frame) & (key_frame < limit)
    mask[...] = seen.astype(jnp.float32)


def weight_part(left, right, part, chunk):
    width = right.shape[1] // CHUNKS
    columns = pl.ds(chunk * width, width)
    ahead = (left.shape[1] // TILE).bit_length() - 1
    blocks = part.shape[ahead:-2]

    def tile(place):
        value = contract(left[:, aligned(place * TILE, TILE)], right[:, columns], TN)
        value = value.reshape(blocks + (part.shape[-2], width)).astype(jnp.bfloat16)
        bits = tuple(lax.rem(lax.div(place, 1 << (ahead - 1 - i)), 2) for i in range(ahead))
        part[bits + (slice(None),) * (len(blocks) + 1) + (columns,)] = value

    over(left.shape[1] // TILE, tile)


def world_kernel(
    digits,
    sides,
    valid,
    counts,
    cotangent,
    pillar_gain,
    space_gain,
    time_gain,
    *refs,
):
    weights_far, refs = refs[:7], refs[7:]
    (pillar_out, latent_out), refs = refs[:2], refs[2:]
    weights, refs = refs[:7], refs[7:]
    weight_sem, refs = refs[0], refs[1:]
    (features, before, hidden, stream, work, joined, mixed, spaced), refs = refs[:8], refs[8:]
    (tile_stream, tile_cot, joined_grad, tile_grad, back, wide, mask, tile_joined), refs = (
        refs[:8],
        refs[8:],
    )
    ways, refs = refs[:6], refs[6:]
    stages = len(digits)
    part_a, part_b = refs[:2]
    scratch = refs[2:]
    sums_a, sums_b = scratch[: stages - 1], scratch[stages - 1 : 2 * stages - 2]
    rest = scratch[2 * stages - 2 :]
    landed_a, landed_b = rest[:stages], rest[stages : 2 * stages]
    send_a, recv_a, send_b, recv_b = rest[2 * stages :]
    orders = halving_orders(digits)
    latent_sum = Halving(
        digits, orders[0], CHUNKS, part_a, sums_a, landed_a, latent_out, send_a, recv_a
    )
    pillar_sum = Halving(
        digits, orders[1], CHUNKS, part_b, sums_b, landed_b, pillar_out, send_b, recv_b
    )
    own_cot = cotangent.at[lax.axis_index("grp")]
    cot_way = Exchange(sides, own_cot, tile_cot, ways[0], ways[1])
    stream_way = Exchange(sides, spaced, tile_stream, ways[2], ways[3])
    back_way = Exchange(sides, tile_grad, back, ways[4], ways[5])

    loads = [
        pltpu.make_async_copy(far, near, weight_sem.at[place])
        for place, (far, near) in enumerate(zip(weights_far, weights))
    ]
    for load in loads:
        load.start()

    barrier = pltpu.get_barrier_semaphore()

    def greet_frame(place):
        device = cot_way.device(cot_way.away(place + 1))
        pl.semaphore_signal(barrier, inc=1, device_id=device, device_id_type=MESH)

    over(FRAMES - 1, greet_frame)
    others = [
        digit
        for digit in digits
        if digit[0] == "dp" or (digit[0] == "seq" and digit[1] >= FRAMES // sides)
    ]
    for digit in others:
        pl.semaphore_signal(barrier, inc=1, device_id=partner(digit), device_id_type=MESH)

    def features_rows(rows):
        features[rows, :] = jnp.log(1.0 + counts[rows, :].astype(jnp.float32)).astype(jnp.bfloat16)

    over_rows(features, features_rows)
    pl.semaphore_wait(barrier, FRAMES - 1 + len(others))
    cot_way.start()

    pillar_proj, latent_proj, input_proj, space_project, space_output = weights[:5]
    time_project, time_output = weights[5:]
    loads[0].wait()
    times(features, pillar_proj, into(before))

    def hidden_rows(rows):
        inputs = unit(before[rows, :])[0] * pillar_gain[...]
        bent = jnp.tanh(GELU * (inputs + 0.044715 * inputs * inputs * inputs))
        hidden[rows, :] = (0.5 * inputs * (1.0 + bent)).astype(jnp.bfloat16)

    over_rows(hidden, hidden_rows)
    loads[1].wait()
    times(hidden, latent_proj, into(work))
    loads[2].wait()
    times(work, input_proj, into(stream))
    norm_rows(stream, space_gain, work)
    loads[3].wait()
    times(work, space_project, into(joined))
    attend(joined, mixed)
    loads[4].wait()

    def space_store(columns, value):
        spaced[:, columns] = (stream[:, columns].astype(jnp.float32) + value).astype(jnp.bfloat16)

    times(mixed, space_output, space_store)
    stream_way.start()

    visible(mask, valid, sides)
    cot_way.wait()
    loads[5].wait()
    loads[6].wait()
    times_back(tile_cot, time_output, into(mixed))
    stream_way.wait()
    norm_rows(tile_stream, time_gain, work)
    times(work, time_project, into(tile_joined))
    attend_back(tile_joined, mixed, joined_grad, mask)
    times_back(joined_grad, time_project, into(work))
    norm_rows_back(tile_stream, time_gain, work, tile_cot, tile_grad)
    back_way.start()

    back_way.wait()
    times_back(back, space_output, into(mixed))
    attend_back(joined, mixed, joined_grad, None)
    times_back(joined_grad, space_project, into(work))
    norm_rows_back(stream, space_gain, work, back, mixed)
    times_back(mixed, input_proj, into(work))
    for chunk in range(CHUNKS):
        weight_part(hidden, work, part_a, chunk)
        latent_sum.start(0, chunk)
    times_back(work, latent_proj, into(wide))

    def before_rows(rows):
        units, scale = unit(before[rows, :])
        inputs = units * pillar_gain[...]
        square = inputs * inputs
        bent = jnp.tanh(GELU * (inputs + 0.044715 * square * inputs))
        slope = 0.5 * (1.0 + bent) + 0.5 * inputs * (1.0 - bent * bent) * GELU * (
            1.0 + 3 * 0.044715 * square
        )
        grad = wide[rows, :] * slope * pillar_gain[...]
        mixed[rows, :] = unit_back(grad, units, scale).astype(jnp.bfloat16)

    over_rows(before, before_rows)
    for chunk in range(CHUNKS):
        weight_part(features, mixed, part_b, chunk)
        pillar_sum.start(0, chunk)
    for stage in range(stages):
        for chunk in range(CHUNKS):
            latent_sum.take(stage, chunk)
            pillar_sum.take(stage, chunk)
    for way in (cot_way, stream_way, back_way):
        way.finish()
    latent_sum.finish()
    pillar_sum.finish()


def shards(
    sizes,
    counts,
    valid_frames,
    cotangent,
    pillar_proj,
    pillar_gain,
    latent_proj,
    input_proj,
    space_gain,
    space_project,
    space_output,
    time_gain,
    time_project,
    time_output,
):
    digits = bit_axes(sizes)
    tokens, width = counts.shape[-2:]
    model = input_proj.shape[1]
    rows = pillar_proj.shape[0] >> len(digits)
    weights = (
        pillar_proj,
        latent_proj,
        input_proj,
        space_project,
        space_output,
        time_project,
        time_output,
    )

    def half(*shape):
        return pltpu.VMEM(shape, jnp.bfloat16)

    def full(*shape):
        return pltpu.VMEM(shape, jnp.float32)

    hidden_width, latent_width = latent_proj.shape
    joined_width = space_project.shape[1]
    shapes = buffer_shapes(digits, rows, latent_width)
    shaped = (2,) * len(digits) + (rows, latent_width)
    scratch = [half(*weight.shape) for weight in weights]
    scratch += [pltpu.SemaphoreType.DMA((len(weights),))]
    scratch += [
        half(tokens, width),
        full(tokens, hidden_width),
        half(tokens, hidden_width),
        half(tokens, model),
        half(tokens, model),
        half(tokens, joined_width),
        half(tokens, model),
        half(tokens, model),
        half(tokens, model),
        half(tokens, model),
        half(tokens, joined_width),
        half(tokens, model),
        half(tokens, model),
        full(tokens, hidden_width),
        full(tokens, tokens),
        half(tokens, joined_width),
    ]
    scratch += [pltpu.SemaphoreType.DMA((FRAMES,))] * 6
    scratch += [half(*shaped)] * 2
    scratch += [half(*shape) for shape in shapes[:-1]] * 2
    scratch += [half(*shape) for shape in shapes] * 2
    scratch += [pltpu.SemaphoreType.DMA((len(digits), CHUNKS))] * 4
    vmem = pl.BlockSpec(memory_space=pltpu.VMEM)
    far = pl.BlockSpec(memory_space=pl.ANY)
    return pl.pallas_call(
        functools.partial(world_kernel, digits, dict(sizes)["grp"]),
        out_shape=[
            jax.ShapeDtypeStruct((rows, hidden_width), jnp.float32),
            jax.ShapeDtypeStruct((rows, latent_width), jnp.float32),
        ],
        in_specs=[pl.BlockSpec(memory_space=pltpu.SMEM)] + [vmem] * 5 + [far] * len(weights),
        out_specs=[vmem] * 2,
        scratch_shapes=scratch,
        compiler_params=pltpu.CompilerParams(
            collective_id=0, has_side_effects=True, vmem_limit_bytes=58 << 20
        ),
    )(
        valid_frames,
        counts.reshape(tokens, width),
        cotangent.reshape(cotangent.shape[1:]),
        pillar_gain.reshape(1, -1),
        space_gain.reshape(1, -1),
        time_gain.reshape(1, -1),
        *weights,
    )


def solution(mesh):
    placed = (
        P("dp", "seq", "grp", None, None),
        P(),
        P("dp", "seq", None, None),
        P(),
        P(),
        P(),
        P(),
        P(),
        P(),
        P(),
        P(),
        P(),
        P(),
    )
    sizes = tuple((name, mesh.shape[name]) for name in ("grp", "seq", "dp"))
    return jax.shard_map(
        functools.partial(shards, sizes),
        mesh=mesh,
        in_specs=placed,
        out_specs=(P(("grp", "seq", "dp"), None), P(("grp", "seq", "dp"), None)),
        check_vma=False,
    )
```
